32 devices in a mesh: grp: 2 (over x), tm: 16 (over z, y, core).
Axes of the slice: x: 2, y: 2, z: 4, core: 2. Of those that a mesh axis runs over, the one named last changes fastest.
Arguments:
- series: bfloat16 [32768, 4096], P('grp', 'tm'), parts along dimension 0, may hold values from -8 to 8
- start_block: bfloat16 [32, 16384], replicated, may hold values from -6 to 6
Outputs:
- basis: float32 [32, 32768], P(None, ('grp', 'tm')), parts along dimension 1
- projected: float32 [32, 8192], P(None, ('grp', 'tm')), parts along dimension 1
The draws below stay inside these ranges and needn't reach their ends.
There are 2 independent parts, one for each index of `grp`. The reference program is written for one: setup_inputs(seed, part) draws one part's arguments, and reference() takes and returns one part's arrays. A program takes and returns all parts, laid end to end along the dimension named above; an argument that names none is the same for every part. Nothing has to cross between parts.
All inputs are finite; a program needn't handle non-finite values.
Results may differ from the reference program's by a relative error of at most 0.002.
The reference program's roundings to bfloat16 on the way (of `cusum` and `sparse`) count: a program that leaves them out, or rounds other values in their place, can miss the bound.
Values may be sent and summed in bfloat16 or wider, within the bound.
A program may use at most 128 MiB of HBM per device.

```python
import jax
import jax.numpy as jnp
from jax import lax

SERIES = 16384
VECTORS = 32
ITERS = 2
STEPS = 4096


def draw_series(key, part):
    keys = jax.random.split(key, 4)
    times = jnp.arange(STEPS)
    noise = jax.random.normal(keys[0], (SERIES, STEPS), jnp.float32)
    change_at = jax.random.randint(keys[1], (SERIES, 1), STEPS // 8, STEPS - STEPS // 8)
    height = jax.random.normal(keys[2], (SERIES, 1), jnp.float32) * 0.6
    chosen = (jax.random.uniform(keys[3], (SERIES, 1), jnp.float32) < 0.25).astype(jnp.float32)
    after = (times[None, :] >= change_at).astype(jnp.float32)
    value = noise + height * chosen * after
    return jnp.clip(value, -8.0, 8.0).astype(jnp.bfloat16)


def normal_values(own_key, extent, deviation, most, held_as=jnp.bfloat16):
    drawn = jax.random.normal(own_key, extent, jnp.float32) * deviation
    return jnp.minimum(jnp.maximum(drawn, -most), most).astype(held_as)


def setup_inputs(seed: int = 0, part: int = 0) -> dict:
    key_of = jax.random.split(jax.random.key(seed), 3)
    own_keys = jax.random.split(jax.random.fold_in(key_of[2], part), 3)
    series = draw_series(jax.random.fold_in(jax.random.fold_in(key_of[2], part), 71), part)
    start_block = normal_values(key_of[1], (VECTORS, SERIES), 1.0, 6.0)
    return dict(series=series, start_block=start_block)


THRESH = 1.0

def shifted(gram):
    width = gram.shape[0]
    amount = 1e-05 * jnp.trace(gram) / width + 1e-06
    return gram + amount * jnp.eye(width, dtype=gram.dtype)

def reference(series, start_block):
    size = min(SERIES, 1024)
    steps_f = jnp.float32(STEPS)
    t = jnp.arange(1, STEPS + 1).astype(jnp.float32)
    weight = jnp.where(t < steps_f, jnp.sqrt(steps_f / jnp.maximum(t * (steps_f - t), 1.0)), 0.0)
    frac = t / steps_f

    def transform(rows):
        prefix = jnp.cumsum(rows.astype(jnp.float32), axis=1)
        total = prefix[:, -1:]
        raw = weight[None, :] * (prefix - frac[None, :] * total)
        soft = jnp.sign(raw) * jnp.maximum(jnp.abs(raw) - THRESH, 0.0)
        return (raw.astype(jnp.bfloat16), soft.astype(jnp.bfloat16))
    grouped = series.reshape(SERIES // size, size, STEPS)
    cusum, sparse = lax.map(transform, grouped)
    cusum = cusum.reshape(SERIES, STEPS)
    sparse = sparse.reshape(SERIES, STEPS)
    block = start_block
    basis = start_block.astype(jnp.float32)
    for step in range(ITERS):
        scores = jnp.dot(block.astype(jnp.float32), sparse.astype(jnp.float32), preferred_element_type=jnp.float32).astype(jnp.bfloat16)
        image = lax.dot_general(scores.astype(jnp.float32), sparse.astype(jnp.float32), (((1,), (1,)), ((), ())), preferred_element_type=jnp.float32)
        gram = jnp.dot(image, image.T, precision=lax.Precision.HIGHEST)
        lower = jnp.linalg.cholesky(shifted(gram))
        first = jax.scipy.linalg.solve_triangular(lower, image, lower=True)
        gram_next = jnp.dot(first, first.T, precision=lax.Precision.HIGHEST)
        lower_next = jnp.linalg.cholesky(shifted(gram_next))
        basis = jax.scipy.linalg.solve_triangular(lower_next, first, lower=True)
        block = basis.astype(jnp.bfloat16)
    projected = jnp.dot(block.astype(jnp.float32), cusum.astype(jnp.float32), preferred_element_type=jnp.float32)
    return (basis, projected)
```

```python
import functools

import jax
import jax.numpy as jnp
from jax import lax
from jax.experimental import pallas as pl
from jax.experimental.pallas import tpu as pltpu
from jax.sharding import PartitionSpec as P

ITERS = 2
THRESH = 1.0
LANES = 128
SUB = 8
MESH = pl.DeviceIdType.MESH
HIGHEST = lax.Precision.HIGHEST
NT = (((1,), (1,)), ((), ()))


def remote(src, dst, send_sem, recv_sem, peer):
    return pltpu.make_async_remote_copy(
        src_ref=src, dst_ref=dst, send_sem=send_sem, recv_sem=recv_sem,
        device_id={"tm": peer}, device_id_type=MESH,
    )


def inverse_factor(gram):
    width = gram.shape[0]
    rows = lax.broadcasted_iota(jnp.int32, (width, LANES), 0)
    cols = lax.broadcasted_iota(jnp.int32, (width, LANES), 1)
    eye = (rows == cols).astype(jnp.float32)
    trace = jnp.sum(jnp.sum(gram * eye, axis=1, keepdims=True), axis=0, keepdims=True)
    amount = 1e-05 * trace / width + 1e-06
    work = gram + amount * eye + (cols == rows + width).astype(jnp.float32)
    pivots = jnp.zeros((width, 1), jnp.float32)
    for j in range(width):
        top = work[j : j + 1, :]
        pivot = top[:, j : j + 1]
        column = work[:, j : j + 1]
        below = lax.broadcasted_iota(jnp.int32, (width, 1), 0)
        factor = jnp.where(below > j, column / pivot, 0.0)
        pivots = jnp.where(below == j, pivot, pivots)
        work = work - factor * top
    inverse = pltpu.roll(work, LANES - width, 1) * lax.rsqrt(pivots)
    return inverse[:, :width]


def kernel(n, series_ref, start_ref, tri_ref, corr_ref, weight_ref, basis_ref, proj_ref,
           sparse, cusum, lhs, tot_send, tot_recv, bt_send, bt_recv,
           one_send, one_recv, two_send, two_recv, gram_send, gram_recv, blk,
           tot_ss, tot_rs, bt_ss, bt_rs, one_ss, one_rs, two_ss, two_rs,
           gram_ss, gram_rs, ag_ss, ag_rs, fw_ss, fw_rs):
    total_rows, steps = series_ref.shape
    vectors = start_ref.shape[0]
    share = total_rows // n
    tiles = share // LANES
    half = n // 2
    me = lax.axis_index("tm")
    core = me % 2
    chip = me // 2
    partner = me + 1 - 2 * core

    barrier = pltpu.get_barrier_semaphore()

    @pl.loop(1, n)
    def _(i):
        pl.semaphore_signal(barrier, inc=1, device_id={"tm": (me + i) % n}, device_id_type=MESH)

    ones = jnp.ones((SUB, steps), jnp.bfloat16)
    row8 = lax.broadcasted_iota(jnp.int32, (SUB, LANES), 0)

    @pl.loop(0, n)
    def _(p):
        part = series_ref[pl.ds(pl.multiple_of(p * share, share), share), :]
        sums = lax.dot_general(ones, part, NT, preferred_element_type=jnp.float32)
        tile = jnp.zeros((SUB, LANES), jnp.float32)
        for q in range(tiles):
            tile = jnp.where(row8 == q, sums[:, q * LANES : (q + 1) * LANES], tile)
        tot_send[p] = tile

    pl.semaphore_wait(barrier, n - 1)

    def tot_copy(i):
        p = (me + i) % n
        return remote(tot_send.at[p], tot_recv.at[me], tot_ss.at[p], tot_rs.at[me], p)

    def tot_from(i):
        p = (me + i) % n
        return remote(tot_send.at[p], tot_recv.at[p], tot_ss.at[p], tot_rs.at[p], p)

    pl.loop(1, n)(lambda i: tot_copy(i).start())
    tot_recv[me] = tot_send[me]
    pl.loop(1, n)(lambda i: tot_from(i).wait_recv())

    def running(d, state):
        bt_send[d, 0] = state
        return state + tot_recv[d]

    total = lax.fori_loop(0, n, running, jnp.zeros((SUB, LANES), jnp.float32))

    def bt_copy(i):
        p = (me + i) % n
        return remote(bt_send.at[p], bt_recv.at[me], bt_ss.at[p], bt_rs.at[me], p)

    def bt_from(p):
        return remote(bt_send.at[p], bt_recv.at[p], bt_ss.at[p], bt_rs.at[p], p)

    @pl.loop(1, n)
    def _(i):
        bt_send[(me + i) % n, 1] = total
        bt_copy(i).start()

    bt_send[me, 1] = total
    bt_recv[me] = bt_send[me]

    def pieces(value):
        high = value.astype(jnp.bfloat16).astype(jnp.float32)
        rest = value - high
        mid = rest.astype(jnp.bfloat16).astype(jnp.float32)
        return [high, mid, rest - mid]

    weight = weight_ref[0:1, :]

    @pl.loop(0, n)
    def _(i):
        p = (me + i) % n

        @pl.when(i > 0)
        def _():
            bt_from(p).wait_recv()

        both = bt_recv[p]
        before, whole = pieces(both[0]), pieces(both[1])
        zero = jnp.zeros((SUB, LANES), jnp.float32)
        stack = jnp.concatenate(before + whole + whole + [zero] * 7, axis=0)
        lhs[...] = stack.T.astype(jnp.bfloat16)

        for q in range(tiles):
            rows = pl.ds(pl.multiple_of(p * share + q * LANES, LANES), LANES)
            prefix = jnp.dot(series_ref[rows, :], tri_ref[...], preferred_element_type=jnp.float32)
            prefix += jnp.dot(lhs[...], corr_ref[q], preferred_element_type=jnp.float32)
            raw = weight * prefix
            cusum[rows, :] = raw.astype(jnp.bfloat16)
            soft = raw - jnp.clip(raw, -THRESH, THRESH)
            sparse[rows, :] = soft.astype(jnp.bfloat16)

    def share_of(p):
        return pl.ds(pl.multiple_of(p * share, share), share)

    lane32 = lax.broadcasted_iota(jnp.int32, (vectors, LANES), 1)

    def sum_gram(k, value):
        part = lax.dot_general(value, value, NT, precision=HIGHEST, preferred_element_type=jnp.float32)
        wide = jnp.concatenate([part] * (LANES // vectors), axis=1)
        packed = jnp.zeros((SUB, LANES), jnp.float32)
        lane8 = lax.broadcasted_iota(jnp.int32, (SUB, LANES), 1) // vectors
        for g in range(vectors // SUB):
            packed = jnp.where(lane8 == g, wide[g * SUB : (g + 1) * SUB, :], packed)
        gram_send[k] = packed

        def out(i):
            p = (me + i) % n
            return remote(gram_send.at[k], gram_recv.at[k, me], gram_ss.at[k, p], gram_rs.at[k, me], p)

        def into(i):
            p = (me + i) % n
            return remote(gram_send.at[k], gram_recv.at[k, p], gram_ss.at[k, p], gram_rs.at[k, p], p)

        pl.loop(1, n)(lambda i: out(i).start())
        gram_recv[k, me] = packed
        pl.loop(1, n)(lambda i: into(i).wait_recv())
        full = lax.fori_loop(0, n, lambda d, s: s + gram_recv[k, d], jnp.zeros((SUB, LANES), jnp.float32))
        pl.loop(1, n)(lambda i: out(i).wait_send())
        parts = [full] + [pltpu.roll(full, LANES - g * vectors, 1) for g in range(1, vectors // SUB)]
        return jnp.where(lane32 < vectors, jnp.concatenate(parts, axis=0), 0.0)

    def gathered_dot(step, target):
        def ag_in(i):
            c = (chip + i) % half
            o = 2 * c + core
            return remote(blk.at[step, o], blk.at[step, o], ag_ss.at[step, c], ag_rs.at[step, c], o)

        def fw_out(i):
            c = (chip + i) % half
            o = 2 * c + core
            return remote(blk.at[step, o], blk.at[step, o], fw_ss.at[step, c], fw_rs.at[step, c], partner)

        def fw_in(i):
            c = (chip + i) % half
            o = 2 * c + 1 - core
            return remote(blk.at[step, o], blk.at[step, o], fw_ss.at[step, c], fw_rs.at[step, c], partner)

        def one(i, acc):
            c = (chip + i) % half

            @pl.when(i > 0)
            def _():
                ag_in(i).wait_recv()

            fw_out(i).start()
            o = 2 * c + core
            return acc + jnp.dot(blk[step, o], target[share_of(o), :], preferred_element_type=jnp.float32)

        def other(i, acc):
            c = (chip + i) % half
            fw_in(i).wait_recv()
            o = 2 * c + 1 - core
            return acc + jnp.dot(blk[step, o], target[share_of(o), :], preferred_element_type=jnp.float32)

        acc = lax.fori_loop(0, half, one, jnp.zeros((vectors, steps), jnp.float32))
        acc = lax.fori_loop(0, half, other, acc)
        pl.loop(0, half)(lambda i: fw_out(i).wait_send())
        return acc

    for step in range(ITERS):
        if step == 0:
            def first_scores(p, acc):
                return acc + jnp.dot(
                    start_ref[:, share_of(p)], sparse[share_of(p), :], preferred_element_type=jnp.float32
                )

            scores = lax.fori_loop(0, n, first_scores, jnp.zeros((vectors, steps), jnp.float32))
        else:
            scores = gathered_dot(step - 1, sparse)
        scores = scores.astype(jnp.bfloat16)

        def image_of(p):
            return lax.dot_general(scores, sparse[share_of(p), :], NT, preferred_element_type=jnp.float32)

        def one_copy(i):
            c = (chip + 1 + i) % half
            return remote(one_send.at[c], one_recv.at[step, c], one_ss.at[step, c], one_rs.at[step, c], partner)

        def two_copy(i):
            c = (chip + 1 + i) % half
            return remote(two_send.at[c], two_recv.at[step, chip], two_ss.at[step, c], two_rs.at[step, chip],
                          2 * c + core)

        def two_from(i):
            c = (chip + 1 + i) % half
            return remote(two_send.at[c], two_recv.at[step, c], two_ss.at[step, c], two_rs.at[step, c],
                          2 * c + core)

        @pl.loop(0, half)
        def _(i):
            c = (chip + 1 + i) % half
            one_send[c] = image_of(2 * c + 1 - core)
            one_copy(i).start()

        @pl.loop(0, half - 1)
        def _(i):
            c = (chip + 1 + i) % half
            own = image_of(2 * c + core)
            one_copy(i).wait_recv()
            two_send[c] = own + one_recv[step, c]
            two_copy(i).start()

        own = image_of(2 * chip + core)
        one_copy(half - 1).wait_recv()
        two_send[chip] = own + one_recv[step, chip]

        def add(i, acc):
            c = (chip + 1 + i) % half
            two_from(i).wait_recv()
            return acc + two_recv[step, c]

        image = lax.fori_loop(0, half - 1, add, two_send[chip])
        pl.loop(0, half)(lambda i: one_copy(i).wait_send())
        pl.loop(0, half - 1)(lambda i: two_copy(i).wait_send())

        inverse = inverse_factor(sum_gram(2 * step, image))
        first = jnp.dot(inverse, image, precision=HIGHEST, preferred_element_type=jnp.float32)
        inverse = inverse_factor(sum_gram(2 * step + 1, first))
        basis = jnp.dot(inverse, first, precision=HIGHEST, preferred_element_type=jnp.float32)
        blk[step, me] = basis.astype(jnp.bfloat16)

        def ag_copy(i):
            c = (chip + i) % half
            return remote(blk.at[step, me], blk.at[step, me], ag_ss.at[step, c], ag_rs.at[step, chip],
                          2 * c + core)

        pl.loop(1, half)(lambda i: ag_copy(i).start())
        if step == ITERS - 1:
            basis_ref[...] = basis
            proj_ref[...] = gathered_dot(step, cusum)
            pl.loop(1, half)(lambda i: ag_copy(i).wait_send())
        else:
            pl.loop(1, half)(lambda i: ag_copy(i).wait_send())

    pl.loop(1, n)(lambda i: tot_copy(i).wait_send())
    pl.loop(1, n)(lambda i: bt_copy(i).wait_send())


def body(series, start_block):
    series_count, blocks = series.shape
    vectors = start_block.shape[0]
    n = lax.axis_size("tm")
    place = lax.axis_index("tm")
    share = series_count // n
    tiles = share // LANES
    half = n // 2
    row_id = lax.broadcasted_iota(jnp.int32, (blocks, blocks), 0)
    col_id = lax.broadcasted_iota(jnp.int32, (blocks, blocks), 1)
    triangle = (row_id <= col_id).astype(jnp.bfloat16)
    steps_f = jnp.float32(blocks * n)
    t_local = (place * blocks + jnp.arange(1, blocks + 1, dtype=jnp.int32)).astype(jnp.float32)
    weight = jnp.where(
        t_local < steps_f, jnp.sqrt(steps_f / jnp.maximum(t_local * (steps_f - t_local), 1.0)), 0.0
    )
    coarse = (place * blocks).astype(jnp.float32) / steps_f
    coarse = jnp.full((blocks,), 1.0, jnp.float32) * coarse
    fine = jnp.arange(1, blocks + 1, dtype=jnp.int32).astype(jnp.float32) / steps_f
    one = jnp.ones((blocks,), jnp.float32)
    none = jnp.zeros((blocks,), jnp.float32)
    kinds = jnp.stack([one] * 3 + [-coarse] * 3 + [-fine] * 3 + [none] * 7)
    pick = jnp.eye(SUB, dtype=jnp.float32)[:tiles]
    corr = (pick[:, None, :, None] * kinds[None, :, None, :]).reshape(tiles, LANES, blocks)
    corr = corr.astype(jnp.bfloat16)
    weight8 = jnp.broadcast_to(weight[None, :], (SUB, blocks))

    f32, bf16 = jnp.float32, jnp.bfloat16
    vmem = pl.BlockSpec(memory_space=pltpu.VMEM)
    dma = pltpu.SemaphoreType.DMA
    return pl.pallas_call(
        functools.partial(kernel, n),
        out_shape=(
            jax.ShapeDtypeStruct((vectors, share), f32),
            jax.ShapeDtypeStruct((vectors, blocks), f32),
        ),
        in_specs=[vmem] * 5,
        out_specs=(vmem, vmem),
        scratch_shapes=[
            pltpu.VMEM((series_count, blocks), bf16),
            pltpu.VMEM((series_count, blocks), bf16),
            pltpu.VMEM((LANES, LANES), bf16),
            pltpu.VMEM((n, SUB, LANES), f32),
            pltpu.VMEM((n, SUB, LANES), f32),
            pltpu.VMEM((n, 2, SUB, LANES), f32),
            pltpu.VMEM((n, 2, SUB, LANES), f32),
            pltpu.VMEM((half, vectors, share), f32),
            pltpu.VMEM((ITERS, half, vectors, share), f32),
            pltpu.VMEM((half, vectors, share), f32),
            pltpu.VMEM((ITERS, half, vectors, share), f32),
            pltpu.VMEM((2 * ITERS, SUB, LANES), f32),
            pltpu.VMEM((2 * ITERS, n, SUB, LANES), f32),
            pltpu.VMEM((ITERS, n, vectors, share), bf16),
            dma((n,)), dma((n,)), dma((n,)), dma((n,)),
            dma((ITERS, half)), dma((ITERS, half)), dma((ITERS, half)), dma((ITERS, half)),
            dma((2 * ITERS, n)), dma((2 * ITERS, n)),
            dma((ITERS, half)), dma((ITERS, half)), dma((ITERS, half)), dma((ITERS, half)),
        ],
        compiler_params=pltpu.CompilerParams(
            collective_id=0, has_side_effects=True, vmem_limit_bytes=56 * 1024 * 1024
        ),
        cost_estimate=pl.CostEstimate(
            flops=2 * series_count * blocks * (blocks + 6 * vectors), bytes_accessed=series_count * blocks * 2,
            transcendentals=0,
        ),
    )(series, start_block, triangle, corr, weight8)


def solution(mesh):
    in_specs = (P("grp", "tm"), P())
    out_specs = (P(None, ("grp", "tm")), P(None, ("grp", "tm")))
    return jax.shard_map(body, mesh=mesh, in_specs=in_specs, out_specs=out_specs, check_vma=False)
```

```python
import functools

import jax
import jax.numpy as jnp
from jax import lax
from jax.experimental import pallas as pl
from jax.experimental.pallas import tpu as pltpu
from jax.sharding import PartitionSpec as P

ITERS = 2
THRESH = 1.0
LANES = 128
SUB = 8
MESH = pl.DeviceIdType.MESH
HIGHEST = lax.Precision.HIGHEST
NT = (((1,), (1,)), ((), ()))


def remote(src, dst, send_sem, recv_sem, peer):
    return pltpu.make_async_remote_copy(
        src_ref=src, dst_ref=dst, send_sem=send_sem, recv_sem=recv_sem,
        device_id={"tm": peer}, device_id_type=MESH,
    )


def inverse_factor(gram):
    width = gram.shape[0]
    rows = lax.broadcasted_iota(jnp.int32, (width, LANES), 0)
    cols = lax.broadcasted_iota(jnp.int32, (width, LANES), 1)
    eye = (rows == cols).astype(jnp.float32)
    trace = jnp.sum(jnp.sum(gram * eye, axis=1, keepdims=True), axis=0, keepdims=True)
    amount = 1e-05 * trace / width + 1e-06
    work = gram + amount * eye + (cols == rows + width).astype(jnp.float32)
    pivots = jnp.zeros((width, 1), jnp.float32)
    for j in range(width):
        top = work[j : j + 1, :]
        pivot = top[:, j : j + 1]
        column = work[:, j : j + 1]
        below = lax.broadcasted_iota(jnp.int32, (width, 1), 0)
        factor = jnp.where(below > j, column / pivot, 0.0)
        pivots = jnp.where(below == j, pivot, pivots)
        work = work - factor * top
    inverse = pltpu.roll(work, LANES - width, 1) * lax.rsqrt(pivots)
    return inverse[:, :width]


def kernel(n, inner, series_ref, start_ref, basis_ref, proj_ref,
           sparse, cusum, lhs, tri_ref, corr_ref, tot_send, tot_recv, bt_send, bt_recv,
           one_send, one_recv, near_send, near_recv, far_send, far_recv, gram_send, gram_recv, blk,
           tot_ss, tot_rs, bt_ss, bt_rs, one_ss, one_rs, near_ss, near_rs,
           far_ss, far_rs, gram_ss, gram_rs, ag_ss, ag_rs, row_ss, row_rs, fw_ss, fw_rs):
    total_rows, steps = series_ref.shape
    vectors = start_ref.shape[0]
    share = total_rows // n
    tiles = share // LANES
    half = n // 2
    me = lax.axis_index("tm")
    core = me % 2
    chip = me // 2
    partner = me + 1 - 2 * core
    outer = half // inner
    near = chip % inner
    far = chip // inner

    def device(a, b, side):
        return 2 * (a * inner + b) + side

    barrier = pltpu.get_barrier_semaphore()

    @pl.loop(1, n)
    def _(i):
        pl.semaphore_signal(barrier, inc=1, device_id={"tm": (me + i) % n}, device_id_type=MESH)

    steps_f = jnp.float32(steps * n)
    tri_rows = lax.broadcasted_iota(jnp.int32, (steps, steps), 0)
    tri_cols = lax.broadcasted_iota(jnp.int32, (steps, steps), 1)
    tri_ref[...] = (tri_rows <= tri_cols).astype(jnp.float32).astype(jnp.bfloat16)
    step_id = lax.broadcasted_iota(jnp.int32, (1, steps), 1) + 1
    t_local = (me * steps + step_id).astype(jnp.float32)
    weight = jnp.where(
        t_local < steps_f, jnp.sqrt(steps_f / jnp.maximum(t_local * (steps_f - t_local), 1.0)), 0.0
    )
    coarse = -(jnp.zeros((1, steps), jnp.int32) + me * steps).astype(jnp.float32) / steps_f
    fine = -step_id.astype(jnp.float32) / steps_f
    kind = lax.broadcasted_iota(jnp.int32, (LANES, steps), 0)
    values = jnp.where(kind < 3 * SUB, 1.0, jnp.where(kind < 6 * SUB, coarse, fine))
    for q in range(tiles):
        used = (kind % SUB == q) & (kind < 9 * SUB)
        corr_ref[q] = jnp.where(used, values, 0.0).astype(jnp.bfloat16)

    ones = jnp.ones((SUB, steps), jnp.bfloat16)
    row8 = lax.broadcasted_iota(jnp.int32, (SUB, LANES), 0)

    @pl.loop(0, n)
    def _(p):
        part = series_ref[pl.ds(pl.multiple_of(p * share, share), share), :]
        sums = lax.dot_general(ones, part, NT, preferred_element_type=jnp.float32)
        tile = jnp.zeros((SUB, LANES), jnp.float32)
        for q in range(tiles):
            tile = jnp.where(row8 == q, sums[:, q * LANES : (q + 1) * LANES], tile)
        tot_send[p] = tile

    pl.semaphore_wait(barrier, n - 1)

    def tot_copy(i):
        p = (me + i) % n
        return remote(tot_send.at[p], tot_recv.at[me], tot_ss.at[p], tot_rs.at[me], p)

    def tot_from(i):
        p = (me + i) % n
        return remote(tot_send.at[p], tot_recv.at[p], tot_ss.at[p], tot_rs.at[p], p)

    pl.loop(1, n)(lambda i: tot_copy(i).start())
    tot_recv[me] = tot_send[me]
    pl.loop(1, n)(lambda i: tot_from(i).wait_recv())

    def running(d, state):
        bt_send[d, 0] = state
        return state + tot_recv[d]

    total = lax.fori_loop(0, n, running, jnp.zeros((SUB, LANES), jnp.float32))

    def bt_copy(i):
        p = (me + i) % n
        return remote(bt_send.at[p], bt_recv.at[me], bt_ss.at[p], bt_rs.at[me], p)

    def bt_from(p):
        return remote(bt_send.at[p], bt_recv.at[p], bt_ss.at[p], bt_rs.at[p], p)

    @pl.loop(1, n)
    def _(i):
        bt_send[(me + i) % n, 1] = total
        bt_copy(i).start()

    bt_send[me, 1] = total
    bt_recv[me] = bt_send[me]

    def pieces(value):
        high = value.astype(jnp.bfloat16).astype(jnp.float32)
        rest = value - high
        mid = rest.astype(jnp.bfloat16).astype(jnp.float32)
        return [high, mid, rest - mid]

    @pl.loop(0, n)
    def _(i):
        p = (me + i) % n

        @pl.when(i > 0)
        def _():
            bt_from(p).wait_recv()

        both = bt_recv[p]
        before, whole = pieces(both[0]), pieces(both[1])
        zero = jnp.zeros((SUB, LANES), jnp.float32)
        stack = jnp.concatenate(before + whole + whole + [zero] * 7, axis=0)
        lhs[...] = stack.T.astype(jnp.bfloat16)

        for q in range(tiles):
            rows = pl.ds(pl.multiple_of(p * share + q * LANES, LANES), LANES)
            prefix = jnp.dot(series_ref[rows, :], tri_ref[...], preferred_element_type=jnp.float32)
            prefix += jnp.dot(lhs[...], corr_ref[q], preferred_element_type=jnp.float32)
            raw = weight * prefix
            cusum[rows, :] = raw.astype(jnp.bfloat16)
            soft = raw - jnp.clip(raw, -THRESH, THRESH)
            sparse[rows, :] = soft.astype(jnp.bfloat16)

    def share_of(p):
        return pl.ds(pl.multiple_of(p * share, share), share)

    lane32 = lax.broadcasted_iota(jnp.int32, (vectors, LANES), 1)

    def sum_gram(k, value):
        part = lax.dot_general(value, value, NT, precision=HIGHEST, preferred_element_type=jnp.float32)
        wide = jnp.concatenate([part] * (LANES // vectors), axis=1)
        packed = jnp.zeros((SUB, LANES), jnp.float32)
        lane8 = lax.broadcasted_iota(jnp.int32, (SUB, LANES), 1) // vectors
        for g in range(vectors // SUB):
            packed = jnp.where(lane8 == g, wide[g * SUB : (g + 1) * SUB, :], packed)
        gram_send[k] = packed

        def out(i):
            p = (me + i) % n
            return remote(gram_send.at[k], gram_recv.at[k, me], gram_ss.at[k, p], gram_rs.at[k, me], p)

        def into(i):
            p = (me + i) % n
            return remote(gram_send.at[k], gram_recv.at[k, p], gram_ss.at[k, p], gram_rs.at[k, p], p)

        pl.loop(1, n)(lambda i: out(i).start())
        gram_recv[k, me] = packed
        pl.loop(1, n)(lambda i: into(i).wait_recv())
        full = lax.fori_loop(0, n, lambda d, s: s + gram_recv[k, d], jnp.zeros((SUB, LANES), jnp.float32))
        pl.loop(1, n)(lambda i: out(i).wait_send())
        parts = [full] + [pltpu.roll(full, LANES - g * vectors, 1) for g in range(1, vectors // SUB)]
        return jnp.where(lane32 < vectors, jnp.concatenate(parts, axis=0), 0.0)

    def gathered_dot(step, target):
        def along(i):
            return (far + i) % outer

        def across(k):
            return (near + k) % inner

        def ag_in(i):
            o = device(along(i), near, core)
            return remote(blk.at[step, o], blk.at[step, o], ag_ss.at[step, along(i)], ag_rs.at[step, along(i)], o)

        def row_out(i, k):
            o = device(along(i), near, core)
            return remote(blk.at[step, o], blk.at[step, o], row_ss.at[step, along(i), across(k)],
                          row_rs.at[step, along(i), near], device(far, across(k), core))

        def row_in(i, k):
            o = device(along(i), across(k), core)
            return remote(blk.at[step, o], blk.at[step, o], row_ss.at[step, along(i), across(k)],
                          row_rs.at[step, along(i), across(k)], device(far, across(k), core))

        def forward(i, k, side):
            a, b = along(i), across(k)
            o = device(a, b, side)
            return remote(blk.at[step, o], blk.at[step, o], fw_ss.at[step, a, b], fw_rs.at[step, a, b], partner)

        def add(acc, o):
            return acc + jnp.dot(blk[step, o], target[share_of(o), :], preferred_element_type=jnp.float32)

        def one(i, acc):
            @pl.when(i > 0)
            def _():
                ag_in(i).wait_recv()

            pl.loop(1, inner)(lambda k: row_out(i, k).start())
            forward(i, 0, core).start()
            return add(acc, device(along(i), near, core))

        def two(i, acc):
            def inner_two(k, acc):
                row_in(i, k).wait_recv()
                forward(i, k, core).start()
                return add(acc, device(along(i), across(k), core))

            return lax.fori_loop(1, inner, inner_two, acc)

        def other(i, acc):
            def inner_other(k, acc):
                forward(i, k, 1 - core).wait_recv()
                return add(acc, device(along(i), across(k), 1 - core))

            return lax.fori_loop(0, inner, inner_other, acc)

        acc = lax.fori_loop(0, outer, one, jnp.zeros((vectors, steps), jnp.float32))
        acc = lax.fori_loop(0, outer, two, acc)
        acc = lax.fori_loop(0, outer, other, acc)

        @pl.loop(0, outer)
        def _(i):
            pl.loop(1, inner)(lambda k: row_out(i, k).wait_send())
            pl.loop(0, inner)(lambda k: forward(i, k, core).wait_send())

        return acc

    for step in range(ITERS):
        if step == 0:
            def first_scores(p, acc):
                return acc + jnp.dot(
                    start_ref[:, share_of(p)], sparse[share_of(p), :], preferred_element_type=jnp.float32
                )

            scores = lax.fori_loop(0, n, first_scores, jnp.zeros((vectors, steps), jnp.float32))
        else:
            scores = gathered_dot(step - 1, sparse)
        scores = scores.astype(jnp.bfloat16)

        def image_of(p):
            return lax.dot_general(scores, sparse[share_of(p), :], NT, preferred_element_type=jnp.float32)

        def along(i):
            return (far + 1 + i) % outer

        def across(k):
            return (near + k) % inner

        def one_copy(i, k):
            a, b = along(i), across(k)
            return remote(one_send.at[a, b], one_recv.at[step, a, b], one_ss.at[step, a, b],
                          one_rs.at[step, a, b], partner)

        def near_copy(i, k):
            a, b = along(i), across(k)
            return remote(near_send.at[a, b], near_recv.at[step, a, near], near_ss.at[step, a, b],
                          near_rs.at[step, a, near], device(far, b, core))

        def near_from(i, k):
            a, b = along(i), across(k)
            return remote(near_send.at[a, b], near_recv.at[step, a, b], near_ss.at[step, a, b],
                          near_rs.at[step, a, b], device(far, b, core))

        def far_copy(i):
            a = along(i)
            return remote(far_send.at[a], far_recv.at[step, far], far_ss.at[step, a], far_rs.at[step, far],
                          device(a, near, core))

        def far_from(i):
            a = along(i)
            return remote(far_send.at[a], far_recv.at[step, a], far_ss.at[step, a], far_rs.at[step, a],
                          device(a, near, core))

        @pl.loop(0, outer)
        def _(i):
            @pl.loop(0, inner)
            def _(j):
                k = (j + 1) % inner
                one_send[along(i), across(k)] = image_of(device(along(i), across(k), 1 - core))
                one_copy(i, k).start()

        @pl.loop(0, outer)
        def _(i):
            @pl.loop(1, inner)
            def _(k):
                own = image_of(device(along(i), across(k), core))
                one_copy(i, k).wait_recv()
                near_send[along(i), across(k)] = own + one_recv[step, along(i), across(k)]
                near_copy(i, k).start()

            own = image_of(device(along(i), near, core))
            one_copy(i, 0).wait_recv()
            far_send[along(i)] = own + one_recv[step, along(i), near]

        def gather_near(i):
            def add(k, acc):
                near_from(i, k).wait_recv()
                return acc + near_recv[step, along(i), across(k)]

            return lax.fori_loop(1, inner, add, far_send[along(i)])

        @pl.loop(0, outer - 1)
        def _(i):
            far_send[along(i)] = gather_near(i)
            far_copy(i).start()

        def add(i, acc):
            far_from(i).wait_recv()
            return acc + far_recv[step, along(i)]

        image = lax.fori_loop(0, outer - 1, add, gather_near(outer - 1))

        @pl.loop(0, outer)
        def _(i):
            pl.loop(0, inner)(lambda k: one_copy(i, k).wait_send())
            pl.loop(1, inner)(lambda k: near_copy(i, k).wait_send())

        pl.loop(0, outer - 1)(lambda i: far_copy(i).wait_send())

        inverse = inverse_factor(sum_gram(2 * step, image))
        first = jnp.dot(inverse, image, precision=HIGHEST, preferred_element_type=jnp.float32)
        inverse = inverse_factor(sum_gram(2 * step + 1, first))
        basis = jnp.dot(inverse, first, precision=HIGHEST, preferred_element_type=jnp.float32)
        blk[step, me] = basis.astype(jnp.bfloat16)

        def ag_copy(i):
            a = (far + i) % outer
            return remote(blk.at[step, me], blk.at[step, me], ag_ss.at[step, a], ag_rs.at[step, far],
                          device(a, near, core))

        pl.loop(1, outer)(lambda i: ag_copy(i).start())
        if step == ITERS - 1:
            basis_ref[...] = basis
            proj_ref[...] = gathered_dot(step, cusum)
            pl.loop(1, outer)(lambda i: ag_copy(i).wait_send())
        else:
            pl.loop(1, outer)(lambda i: ag_copy(i).wait_send())

    pl.loop(1, n)(lambda i: tot_copy(i).wait_send())
    pl.loop(1, n)(lambda i: bt_copy(i).wait_send())


def body(series, start_block):
    series_count, blocks = series.shape
    vectors = start_block.shape[0]
    n = lax.axis_size("tm")
    share = series_count // n
    tiles = share // LANES
    half = n // 2
    inner = 1
    while 4 * inner * inner <= half:
        inner *= 2
    outer = half // inner

    f32, bf16 = jnp.float32, jnp.bfloat16
    vmem = pl.BlockSpec(memory_space=pltpu.VMEM)
    dma = pltpu.SemaphoreType.DMA
    return pl.pallas_call(
        functools.partial(kernel, n, inner),
        out_shape=(
            jax.ShapeDtypeStruct((vectors, share), f32),
            jax.ShapeDtypeStruct((vectors, blocks), f32),
        ),
        in_specs=[vmem] * 2,
        out_specs=(vmem, vmem),
        scratch_shapes=[
            pltpu.VMEM((series_count, blocks), bf16),
            pltpu.VMEM((series_count, blocks), bf16),
            pltpu.VMEM((LANES, LANES), bf16),
            pltpu.VMEM((blocks, blocks), bf16),
            pltpu.VMEM((tiles, LANES, blocks), bf16),
            pltpu.VMEM((n, SUB, LANES), f32),
            pltpu.VMEM((n, SUB, LANES), f32),
            pltpu.VMEM((n, 2, SUB, LANES), f32),
            pltpu.VMEM((n, 2, SUB, LANES), f32),
            pltpu.VMEM((outer, inner, vectors, share), f32),
            pltpu.VMEM((ITERS, outer, inner, vectors, share), f32),
            pltpu.VMEM((outer, inner, vectors, share), f32),
            pltpu.VMEM((ITERS, outer, inner, vectors, share), f32),
            pltpu.VMEM((outer, vectors, share), f32),
            pltpu.VMEM((ITERS, outer, vectors, share), f32),
            pltpu.VMEM((2 * ITERS, SUB, LANES), f32),
            pltpu.VMEM((2 * ITERS, n, SUB, LANES), f32),
            pltpu.VMEM((ITERS, n, vectors, share), bf16),
            dma((n,)), dma((n,)), dma((n,)), dma((n,)),
            dma((ITERS, outer, inner)), dma((ITERS, outer, inner)),
            dma((ITERS, outer, inner)), dma((ITERS, outer, inner)),
            dma((ITERS, outer)), dma((ITERS, outer)),
            dma((2 * ITERS, n)), dma((2 * ITERS, n)),
            dma((ITERS, outer)), dma((ITERS, outer)),
            dma((ITERS, outer, inner)), dma((ITERS, outer, inner)),
            dma((ITERS, outer, inner)), dma((ITERS, outer, inner)),
        ],
        compiler_params=pltpu.CompilerParams(
            collective_id=0, has_side_effects=True, vmem_limit_bytes=56 * 1024 * 1024
        ),
        cost_estimate=pl.CostEstimate(
            flops=2 * series_count * blocks * (blocks + 6 * vectors), bytes_accessed=series_count * blocks * 2,
            transcendentals=0,
        ),
    )(series, start_block)


def solution(mesh):
    in_specs = (P("grp", "tm"), P())
    out_specs = (P(None, ("grp", "tm")), P(None, ("grp", "tm")))
    return jax.shard_map(body, mesh=mesh, in_specs=in_specs, out_specs=out_specs, check_vma=False)
```

```python
import functools

import jax
import jax.numpy as jnp
from jax import lax
from jax.experimental import pallas as pl
from jax.experimental.pallas import tpu as pltpu
from jax.sharding import PartitionSpec as P

ITERS = 2
THRESH = 1.0
LANES = 128
SUB = 8
MESH = pl.DeviceIdType.MESH
HIGHEST = lax.Precision.HIGHEST
NT = (((1,), (1,)), ((), ()))


def remote(src, dst, send_sem, recv_sem, peer):
    return pltpu.make_async_remote_copy(
        src_ref=src, dst_ref=dst, send_sem=send_sem, recv_sem=recv_sem,
        device_id={"tm": peer}, device_id_type=MESH,
    )


def each(low, high, run):
    if high - low <= 16:
        for i in range(low, high):
            run(i)
    else:
        pl.loop(low, high)(run)


def inverse_factor(gram):
    width = gram.shape[0]
    rows = lax.broadcasted_iota(jnp.int32, (width, LANES), 0)
    cols = lax.broadcasted_iota(jnp.int32, (width, LANES), 1)
    eye = (rows == cols).astype(jnp.float32)
    trace = jnp.sum(jnp.sum(gram * eye, axis=1, keepdims=True), axis=0, keepdims=True)
    amount = 1e-05 * trace / width + 1e-06
    work = gram + amount * eye + (cols == rows + width).astype(jnp.float32)
    pivots = jnp.zeros((width, 1), jnp.float32)
    for j in range(width):
        top = work[j : j + 1, :]
        pivot = top[:, j : j + 1]
        column = work[:, j : j + 1]
        below = lax.broadcasted_iota(jnp.int32, (width, 1), 0)
        factor = jnp.where(below > j, column / pivot, 0.0)
        pivots = jnp.where(below == j, pivot, pivots)
        work = work - factor * top
    inverse = pltpu.roll(work, LANES - width, 1) * lax.rsqrt(pivots)
    return inverse[:, :width]


def kernel(n, inner, series_hbm, start_hbm, basis_ref, proj_ref,
           series_ref, start_ref, load_sem, sparse, cusum, lhs, tri_ref, corr_ref, tot_send, tot_recv, bt_send, bt_recv,
           one_send, one_recv, near_send, near_recv, far_send, far_recv, gram_send, gram_recv, blk,
           tot_ss, tot_rs, bt_ss, bt_rs, one_ss, one_rs, near_ss, near_rs,
           far_ss, far_rs, gram_ss, gram_rs, ag_ss, ag_rs, row_ss, row_rs, fw_ss, fw_rs):
    total_rows, steps = series_hbm.shape
    vectors = start_ref.shape[0]
    share = total_rows // n
    tiles = share // LANES
    half = n // 2
    me = lax.axis_index("tm")
    core = me % 2
    chip = me // 2
    partner = me + 1 - 2 * core
    outer = half // inner
    near = chip % inner
    far = chip // inner

    def device(a, b, side):
        return 2 * (a * inner + b) + side

    def load(p):
        rows = pl.ds(pl.multiple_of(p * share, share), share)
        return pltpu.make_async_copy(series_hbm.at[rows, :], series_ref.at[rows, :], load_sem.at[p])

    load_start = pltpu.make_async_copy(start_hbm, start_ref, load_sem.at[n])
    each(0, n, lambda p: load(p).start())
    load_start.start()

    barrier = pltpu.get_barrier_semaphore()

    @pl.loop(1, n)
    def _(i):
        pl.semaphore_signal(barrier, inc=1, device_id={"tm": (me + i) % n}, device_id_type=MESH)

    steps_f = jnp.float32(steps * n)
    tri_rows = lax.broadcasted_iota(jnp.int32, (steps, steps), 0)
    tri_cols = lax.broadcasted_iota(jnp.int32, (steps, steps), 1)
    tri_ref[...] = (tri_rows <= tri_cols).astype(jnp.float32).astype(jnp.bfloat16)
    step_id = lax.broadcasted_iota(jnp.int32, (1, steps), 1) + 1
    t_local = (me * steps + step_id).astype(jnp.float32)
    weight = jnp.where(
        t_local < steps_f, jnp.sqrt(steps_f / jnp.maximum(t_local * (steps_f - t_local), 1.0)), 0.0
    )
    coarse = -(jnp.zeros((1, steps), jnp.int32) + me * steps).astype(jnp.float32) / steps_f
    fine = -step_id.astype(jnp.float32) / steps_f
    kind = lax.broadcasted_iota(jnp.int32, (LANES, steps), 0)
    values = jnp.where(kind < 3 * SUB, 1.0, jnp.where(kind < 6 * SUB, coarse, fine))
    for q in range(tiles):
        used = (kind % SUB == q) & (kind < 9 * SUB)
        corr_ref[q] = jnp.where(used, values, 0.0).astype(jnp.bfloat16)

    ones = jnp.ones((SUB, steps), jnp.bfloat16)
    row8 = lax.broadcasted_iota(jnp.int32, (SUB, LANES), 0)

    @pl.loop(0, n)
    def _(p):
        load(p).wait()
        part = series_ref[pl.ds(pl.multiple_of(p * share, share), share), :]
        sums = lax.dot_general(ones, part, NT, preferred_element_type=jnp.float32)
        tile = jnp.zeros((SUB, LANES), jnp.float32)
        for q in range(tiles):
            tile = jnp.where(row8 == q, sums[:, q * LANES : (q + 1) * LANES], tile)
        tot_send[p] = tile

    pl.semaphore_wait(barrier, n - 1)

    def tot_copy(i):
        p = (me + i) % n
        return remote(tot_send.at[p], tot_recv.at[me], tot_ss.at[p], tot_rs.at[me], p)

    def tot_from(i):
        p = (me + i) % n
        return remote(tot_send.at[p], tot_recv.at[p], tot_ss.at[p], tot_rs.at[p], p)

    each(1, n, lambda i: tot_copy(i).start())
    tot_recv[me] = tot_send[me]
    each(1, n, lambda i: tot_from(i).wait_recv())

    def running(d, state):
        bt_send[d, 0] = state
        return state + tot_recv[d]

    total = lax.fori_loop(0, n, running, jnp.zeros((SUB, LANES), jnp.float32))

    def bt_copy(i):
        p = (me + i) % n
        return remote(bt_send.at[p], bt_recv.at[me], bt_ss.at[p], bt_rs.at[me], p)

    def bt_from(p):
        return remote(bt_send.at[p], bt_recv.at[p], bt_ss.at[p], bt_rs.at[p], p)

    def send_back(i):
        bt_send[(me + i) % n, 1] = total
        bt_copy(i).start()

    each(1, n, send_back)

    bt_send[me, 1] = total
    bt_recv[me] = bt_send[me]

    def pieces(value):
        high = value.astype(jnp.bfloat16).astype(jnp.float32)
        rest = value - high
        mid = rest.astype(jnp.bfloat16).astype(jnp.float32)
        return [high, mid, rest - mid]

    load_start.wait()

    def transform(i, acc):
        p = (me + i) % n

        @pl.when(i > 0)
        def _():
            bt_from(p).wait_recv()

        both = bt_recv[p]
        before, whole = pieces(both[0]), pieces(both[1])
        zero = jnp.zeros((SUB, LANES), jnp.float32)
        stack = jnp.concatenate(before + whole + whole + [zero] * 7, axis=0)
        lhs[...] = stack.T.astype(jnp.bfloat16)

        for q in range(tiles):
            rows = pl.ds(pl.multiple_of(p * share + q * LANES, LANES), LANES)
            prefix = jnp.dot(series_ref[rows, :], tri_ref[...], preferred_element_type=jnp.float32)
            prefix += jnp.dot(lhs[...], corr_ref[q], preferred_element_type=jnp.float32)
            raw = weight * prefix
            cusum[rows, :] = raw.astype(jnp.bfloat16)
            soft = raw - jnp.clip(raw, -THRESH, THRESH)
            soft = soft.astype(jnp.bfloat16)
            sparse[rows, :] = soft
        return acc

    lax.fori_loop(0, n, transform, 0)

    def share_of(p):
        return pl.ds(pl.multiple_of(p * share, share), share)

    late = []
    sent = []
    lane32 = lax.broadcasted_iota(jnp.int32, (vectors, LANES), 1)

    def sum_gram(k, value):
        part = lax.dot_general(value, value, NT, precision=HIGHEST, preferred_element_type=jnp.float32)
        wide = jnp.concatenate([part] * (LANES // vectors), axis=1)
        packed = jnp.zeros((SUB, LANES), jnp.float32)
        lane8 = lax.broadcasted_iota(jnp.int32, (SUB, LANES), 1) // vectors
        for g in range(vectors // SUB):
            packed = jnp.where(lane8 == g, wide[g * SUB : (g + 1) * SUB, :], packed)
        gram_send[k] = packed

        def out(i):
            p = (me + i) % n
            return remote(gram_send.at[k], gram_recv.at[k, me], gram_ss.at[k, p], gram_rs.at[k, me], p)

        def into(i):
            p = (me + i) % n
            return remote(gram_send.at[k], gram_recv.at[k, p], gram_ss.at[k, p], gram_rs.at[k, p], p)

        each(1, n, lambda i: out(i).start())
        gram_recv[k, me] = packed
        each(1, n, lambda i: into(i).wait_recv())
        full = jnp.sum(gram_recv[k], axis=0)
        late.append(lambda: each(1, n, lambda i: out(i).wait_send()))
        parts = [full] + [pltpu.roll(full, LANES - g * vectors, 1) for g in range(1, vectors // SUB)]
        return jnp.where(lane32 < vectors, jnp.concatenate(parts, axis=0), 0.0)

    def gathered_dot(step, target):
        def along(i):
            return (far + i) % outer

        def across(k):
            return (near + k) % inner

        def ag_in(i):
            o = device(along(i), near, core)
            return remote(blk.at[step, o], blk.at[step, o], ag_ss.at[step, along(i)], ag_rs.at[step, along(i)], o)

        def row_out(i, k):
            o = device(along(i), near, core)
            return remote(blk.at[step, o], blk.at[step, o], row_ss.at[step, along(i), across(k)],
                          row_rs.at[step, along(i), near], device(far, across(k), core))

        def row_in(i, k):
            o = device(along(i), across(k), core)
            return remote(blk.at[step, o], blk.at[step, o], row_ss.at[step, along(i), across(k)],
                          row_rs.at[step, along(i), across(k)], device(far, across(k), core))

        def forward(i, k, side):
            a, b = along(i), across(k)
            o = device(a, b, side)
            return remote(blk.at[step, o], blk.at[step, o], fw_ss.at[step, a, b], fw_rs.at[step, a, b], partner)

        def add(acc, o):
            return acc + jnp.dot(blk[step, o], target[share_of(o), :], preferred_element_type=jnp.float32)

        def one(i, acc):
            @pl.when(i > 0)
            def _():
                ag_in(i).wait_recv()

            each(1, inner, lambda k: row_out(i, k).start())
            forward(i, 0, core).start()
            return add(acc, device(along(i), near, core))

        def two(i, acc):
            def inner_two(k, acc):
                row_in(i, k).wait_recv()
                forward(i, k, core).start()
                return add(acc, device(along(i), across(k), core))

            return lax.fori_loop(1, inner, inner_two, acc)

        def other(i, acc):
            def inner_other(k, acc):
                forward(i, k, 1 - core).wait_recv()
                return add(acc, device(along(i), across(k), 1 - core))

            return lax.fori_loop(0, inner, inner_other, acc)

        acc = lax.fori_loop(0, outer, one, jnp.zeros((vectors, steps), jnp.float32))
        acc = lax.fori_loop(0, outer, two, acc)
        acc = lax.fori_loop(0, outer, other, acc)

        def finish():
            @pl.loop(0, outer)
            def _(i):
                each(1, inner, lambda k: row_out(i, k).wait_send())
                each(0, inner, lambda k: forward(i, k, core).wait_send())

        late.append(finish)
        return acc

    for step in range(ITERS):
        if step == 0:
            def first_scores(p, acc):
                return acc + jnp.dot(
                    start_ref[:, share_of(p)], sparse[share_of(p), :], preferred_element_type=jnp.float32
                )

            scores = lax.fori_loop(0, n, first_scores, jnp.zeros((vectors, steps), jnp.float32))
        else:
            scores = gathered_dot(step - 1, sparse)
        scores = scores.astype(jnp.bfloat16)

        def image_of(p):
            return lax.dot_general(scores, sparse[share_of(p), :], NT, preferred_element_type=jnp.float32)

        def along(i):
            return (far + 1 + i) % outer

        def across(k):
            return (near + k) % inner

        def one_copy(i, k, step=step):
            a, b = along(i), across(k)
            return remote(one_send.at[a, b], one_recv.at[step, a, b], one_ss.at[step, a, b],
                          one_rs.at[step, a, b], partner)

        def near_copy(i, k, step=step):
            a, b = along(i), across(k)
            return remote(near_send.at[a, b], near_recv.at[step, a, near], near_ss.at[step, a, b],
                          near_rs.at[step, a, near], device(far, b, core))

        def near_from(i, k):
            a, b = along(i), across(k)
            return remote(near_send.at[a, b], near_recv.at[step, a, b], near_ss.at[step, a, b],
                          near_rs.at[step, a, b], device(far, b, core))

        def far_copy(i, step=step):
            a = along(i)
            return remote(far_send.at[a], far_recv.at[step, far], far_ss.at[step, a], far_rs.at[step, far],
                          device(a, near, core))

        def far_from(i):
            a = along(i)
            return remote(far_send.at[a], far_recv.at[step, a], far_ss.at[step, a], far_rs.at[step, a],
                          device(a, near, core))

        for done in sent:
            done()
        sent.clear()

        @pl.loop(0, outer)
        def _(i):
            @pl.loop(0, inner)
            def _(j):
                k = (j + 1) % inner
                one_send[along(i), across(k)] = image_of(device(along(i), across(k), 1 - core))
                one_copy(i, k).start()

        @pl.loop(0, outer)
        def _(i):
            @pl.loop(1, inner)
            def _(k):
                own = image_of(device(along(i), across(k), core))
                one_copy(i, k).wait_recv()
                near_send[along(i), across(k)] = own + one_recv[step, along(i), across(k)]
                near_copy(i, k).start()

            own = image_of(device(along(i), near, core))
            one_copy(i, 0).wait_recv()
            far_send[along(i)] = own + one_recv[step, along(i), near]

        def gather_near(i):
            def add(k, acc):
                near_from(i, k).wait_recv()
                return acc + near_recv[step, along(i), across(k)]

            return lax.fori_loop(1, inner, add, far_send[along(i)])

        @pl.loop(0, outer - 1)
        def _(i):
            far_send[along(i)] = gather_near(i)
            far_copy(i).start()

        def add(i, acc):
            far_from(i).wait_recv()
            return acc + far_recv[step, along(i)]

        image = lax.fori_loop(0, outer - 1, add, gather_near(outer - 1))

        def finish(one_copy=one_copy, near_copy=near_copy, far_copy=far_copy):
            @pl.loop(0, outer)
            def _(i):
                each(0, inner, lambda k: one_copy(i, k).wait_send())
                each(1, inner, lambda k: near_copy(i, k).wait_send())

            each(0, outer - 1, lambda i: far_copy(i).wait_send())

        sent.append(finish)

        inverse = inverse_factor(sum_gram(2 * step, image))
        first = jnp.dot(inverse, image, precision=HIGHEST, preferred_element_type=jnp.float32)
        inverse = inverse_factor(sum_gram(2 * step + 1, first))
        basis = jnp.dot(inverse, first, precision=HIGHEST, preferred_element_type=jnp.float32)
        blk[step, me] = basis.astype(jnp.bfloat16)

        def ag_copy(i, step=step):
            a = (far + i) % outer
            return remote(blk.at[step, me], blk.at[step, me], ag_ss.at[step, a], ag_rs.at[step, far],
                          device(a, near, core))

        each(1, outer, lambda i: ag_copy(i).start())
        late.append(lambda ag_copy=ag_copy: each(1, outer, lambda i: ag_copy(i).wait_send()))
        if step == ITERS - 1:
            basis_ref[...] = basis
            proj_ref[...] = gathered_dot(step, cusum)

    for done in sent + late:
        done()
    each(1, n, lambda i: tot_copy(i).wait_send())
    each(1, n, lambda i: bt_copy(i).wait_send())


def body(series, start_block):
    series_count, blocks = series.shape
    vectors = start_block.shape[0]
    n = lax.axis_size("tm")
    share = series_count // n
    tiles = share // LANES
    half = n // 2
    inner = 1
    while 4 * inner * inner <= half:
        inner *= 2
    outer = half // inner

    f32, bf16 = jnp.float32, jnp.bfloat16
    vmem = pl.BlockSpec(memory_space=pltpu.VMEM)
    dma = pltpu.SemaphoreType.DMA
    hbm = pl.BlockSpec(memory_space=pl.ANY)
    return pl.pallas_call(
        functools.partial(kernel, n, inner),
        out_shape=(
            jax.ShapeDtypeStruct((vectors, share), f32),
            jax.ShapeDtypeStruct((vectors, blocks), f32),
        ),
        in_specs=[hbm] * 2,
        out_specs=(vmem, vmem),
        scratch_shapes=[
            pltpu.VMEM((series_count, blocks), bf16),
            pltpu.VMEM((vectors, series_count), bf16),
            dma((n + 1,)),
            pltpu.VMEM((series_count, blocks), bf16),
            pltpu.VMEM((series_count, blocks), bf16),
            pltpu.VMEM((LANES, LANES), bf16),
            pltpu.VMEM((blocks, blocks), bf16),
            pltpu.VMEM((tiles, LANES, blocks), bf16),
            pltpu.VMEM((n, SUB, LANES), f32),
            pltpu.VMEM((n, SUB, LANES), f32),
            pltpu.VMEM((n, 2, SUB, LANES), f32),
            pltpu.VMEM((n, 2, SUB, LANES), f32),
            pltpu.VMEM((outer, inner, vectors, share), f32),
            pltpu.VMEM((ITERS, outer, inner, vectors, share), f32),
            pltpu.VMEM((outer, inner, vectors, share), f32),
            pltpu.VMEM((ITERS, outer, inner, vectors, share), f32),
            pltpu.VMEM((outer, vectors, share), f32),
            pltpu.VMEM((ITERS, outer, vectors, share), f32),
            pltpu.VMEM((2 * ITERS, SUB, LANES), f32),
            pltpu.VMEM((2 * ITERS, n, SUB, LANES), f32),
            pltpu.VMEM((ITERS, n, vectors, share), bf16),
            dma((n,)), dma((n,)), dma((n,)), dma((n,)),
            dma((ITERS, outer, inner)), dma((ITERS, outer, inner)),
            dma((ITERS, outer, inner)), dma((ITERS, outer, inner)),
            dma((ITERS, outer)), dma((ITERS, outer)),
            dma((2 * ITERS, n)), dma((2 * ITERS, n)),
            dma((ITERS, outer)), dma((ITERS, outer)),
            dma((ITERS, outer, inner)), dma((ITERS, outer, inner)),
            dma((ITERS, outer, inner)), dma((ITERS, outer, inner)),
        ],
        compiler_params=pltpu.CompilerParams(
            collective_id=0, has_side_effects=True, vmem_limit_bytes=56 * 1024 * 1024
        ),
        cost_estimate=pl.CostEstimate(
            flops=2 * series_count * blocks * (blocks + 6 * vectors), bytes_accessed=series_count * blocks * 2,
            transcendentals=0,
        ),
    )(series, start_block)


def solution(mesh):
    in_specs = (P("grp", "tm"), P())
    out_specs = (P(None, ("grp", "tm")), P(None, ("grp", "tm")))
    return jax.shard_map(body, mesh=mesh, in_specs=in_specs, out_specs=out_specs, check_vma=False)
```

```python
import functools

import jax
import jax.numpy as jnp
from jax import lax
from jax.experimental import pallas as pl
from jax.experimental.pallas import tpu as pltpu
from jax.sharding import PartitionSpec as P

ITERS = 2
THRESH = 1.0
LANES = 128
SUB = 8
MESH = pl.DeviceIdType.MESH
HIGHEST = lax.Precision.HIGHEST
NT = (((1,), (1,)), ((), ()))


def remote(src, dst, send_sem, recv_sem, peer):
    return pltpu.make_async_remote_copy(
        src_ref=src, dst_ref=dst, send_sem=send_sem, recv_sem=recv_sem,
        device_id={"tm": peer}, device_id_type=MESH,
    )


def each(low, high, run):
    if high - low <= 16:
        for i in range(low, high):
            run(i)
    else:
        pl.loop(low, high)(run)


def inverse_factor(gram):
    width = gram.shape[0]
    rows = lax.broadcasted_iota(jnp.int32, (width, LANES), 0)
    cols = lax.broadcasted_iota(jnp.int32, (width, LANES), 1)
    eye = (rows == cols).astype(jnp.float32)
    trace = jnp.sum(jnp.sum(gram * eye, axis=1, keepdims=True), axis=0, keepdims=True)
    amount = 1e-05 * trace / width + 1e-06
    work = gram + amount * eye + (cols == rows + width).astype(jnp.float32)
    pivots = jnp.zeros((width, 1), jnp.float32)
    for j in range(width):
        top = work[j : j + 1, :]
        pivot = top[:, j : j + 1]
        column = work[:, j : j + 1]
        below = lax.broadcasted_iota(jnp.int32, (width, 1), 0)
        factor = jnp.where(below > j, column / pivot, 0.0)
        pivots = jnp.where(below == j, pivot, pivots)
        work = work - factor * top
    inverse = pltpu.roll(work, LANES - width, 1) * lax.rsqrt(pivots)
    return inverse[:, :width]


def kernel(n, inner, series_hbm, start_hbm, basis_ref, proj_ref,
           series_ref, start_ref, load_sem, sparse, cusum, lhs, tri_ref, corr_ref, tot_send, tot_recv, bt_send, bt_recv,
           one_send, one_recv, near_send, near_recv, far_send, far_recv, gram_send, gram_recv, blk,
           tot_ss, tot_rs, bt_ss, bt_rs, one_ss, one_rs, near_ss, near_rs,
           far_ss, far_rs, gram_ss, gram_rs, ag_ss, ag_rs, row_ss, row_rs, fw_ss, fw_rs):
    total_rows, steps = series_hbm.shape
    vectors = start_ref.shape[0]
    share = total_rows // n
    tiles = share // LANES
    half = n // 2
    me = lax.axis_index("tm")
    core = me % 2
    chip = me // 2
    partner = me + 1 - 2 * core
    outer = half // inner
    near = chip % inner
    far = chip // inner

    def device(a, b, side):
        return 2 * (a * inner + b) + side

    def load(p):
        rows = pl.ds(pl.multiple_of(p * share, share), share)
        return pltpu.make_async_copy(series_hbm.at[rows, :], series_ref.at[rows, :], load_sem.at[p])

    load_start = pltpu.make_async_copy(start_hbm, start_ref, load_sem.at[n])
    each(0, n, lambda p: load(p).start())
    load_start.start()

    barrier = pltpu.get_barrier_semaphore()

    @pl.loop(1, n)
    def _(i):
        pl.semaphore_signal(barrier, inc=1, device_id={"tm": (me + i) % n}, device_id_type=MESH)

    steps_f = jnp.float32(steps * n)
    tri_rows = lax.broadcasted_iota(jnp.int32, (steps, steps), 0)
    tri_cols = lax.broadcasted_iota(jnp.int32, (steps, steps), 1)
    tri_ref[...] = (tri_rows <= tri_cols).astype(jnp.float32).astype(jnp.bfloat16)
    step_id = lax.broadcasted_iota(jnp.int32, (1, steps), 1) + 1
    t_local = (me * steps + step_id).astype(jnp.float32)
    weight = jnp.where(
        t_local < steps_f, jnp.sqrt(steps_f / jnp.maximum(t_local * (steps_f - t_local), 1.0)), 0.0
    )
    coarse = -(jnp.zeros((1, steps), jnp.int32) + me * steps).astype(jnp.float32) / steps_f
    fine = -step_id.astype(jnp.float32) / steps_f
    kind = lax.broadcasted_iota(jnp.int32, (LANES, steps), 0)
    values = jnp.where(kind < 3 * SUB, 1.0, jnp.where(kind < 6 * SUB, coarse, fine))
    for q in range(tiles):
        used = (kind % SUB == q) & (kind < 9 * SUB)
        corr_ref[q] = jnp.where(used, values, 0.0).astype(jnp.bfloat16)

    ones = jnp.ones((SUB, steps), jnp.bfloat16)
    row8 = lax.broadcasted_iota(jnp.int32, (SUB, LANES), 0)

    @pl.loop(0, n)
    def _(p):
        load(p).wait()
        part = series_ref[pl.ds(pl.multiple_of(p * share, share), share), :]
        sums = lax.dot_general(ones, part, NT, preferred_element_type=jnp.float32)
        tile = jnp.zeros((SUB, LANES), jnp.float32)
        for q in range(tiles):
            tile = jnp.where(row8 == q, sums[:, q * LANES : (q + 1) * LANES], tile)
        tot_send[p] = tile

    pl.semaphore_wait(barrier, n - 1)

    def tot_copy(i):
        p = (me + i) % n
        return remote(tot_send.at[p], tot_recv.at[me], tot_ss.at[p], tot_rs.at[me], p)

    def tot_from(i):
        p = (me + i) % n
        return remote(tot_send.at[p], tot_recv.at[p], tot_ss.at[p], tot_rs.at[p], p)

    each(1, n, lambda i: tot_copy(i).start())
    tot_recv[me] = tot_send[me]
    each(1, n, lambda i: tot_from(i).wait_recv())

    def running(d, state):
        bt_send[d, 0] = state
        return state + tot_recv[d]

    total = lax.fori_loop(0, n, running, jnp.zeros((SUB, LANES), jnp.float32))

    def bt_copy(i):
        p = (me + i) % n
        return remote(bt_send.at[p], bt_recv.at[me], bt_ss.at[p], bt_rs.at[me], p)

    def bt_from(p):
        return remote(bt_send.at[p], bt_recv.at[p], bt_ss.at[p], bt_rs.at[p], p)

    def send_back(i):
        bt_send[(me + i) % n, 1] = total
        bt_copy(i).start()

    each(1, n, send_back)

    bt_send[me, 1] = total
    bt_recv[me] = bt_send[me]

    def pieces(value):
        high = value.astype(jnp.bfloat16).astype(jnp.float32)
        rest = value - high
        mid = rest.astype(jnp.bfloat16).astype(jnp.float32)
        return [high, mid, rest - mid]

    load_start.wait()

    def transform(i, acc):
        p = (me + i) % n

        @pl.when(i > 0)
        def _():
            bt_from(p).wait_recv()

        both = bt_recv[p]
        before, whole = pieces(both[0]), pieces(both[1])
        zero = jnp.zeros((SUB, LANES), jnp.float32)
        stack = jnp.concatenate(before + whole + whole + [zero] * 7, axis=0)
        lhs[...] = stack.T.astype(jnp.bfloat16)

        for q in range(tiles):
            rows = pl.ds(pl.multiple_of(p * share + q * LANES, LANES), LANES)
            prefix = jnp.dot(series_ref[rows, :], tri_ref[...], preferred_element_type=jnp.float32)
            prefix += jnp.dot(lhs[...], corr_ref[q], preferred_element_type=jnp.float32)
            raw = weight * prefix
            cusum[rows, :] = raw.astype(jnp.bfloat16)
            soft = raw - jnp.clip(raw, -THRESH, THRESH)
            soft = soft.astype(jnp.bfloat16)
            sparse[rows, :] = soft
        return acc

    lax.fori_loop(0, n, transform, 0)

    def share_of(p):
        return pl.ds(pl.multiple_of(p * share, share), share)

    late = []
    sent = []
    lane32 = lax.broadcasted_iota(jnp.int32, (vectors, LANES), 1)

    def sum_gram(k, value):
        part = lax.dot_general(value, value, NT, precision=HIGHEST, preferred_element_type=jnp.float32)
        wide = jnp.concatenate([part] * (LANES // vectors), axis=1)
        packed = jnp.zeros((SUB, LANES), jnp.float32)
        lane8 = lax.broadcasted_iota(jnp.int32, (SUB, LANES), 1) // vectors
        for g in range(vectors // SUB):
            packed = jnp.where(lane8 == g, wide[g * SUB : (g + 1) * SUB, :], packed)
        gram_send[k] = packed

        def out(i):
            p = (me + i) % n
            return remote(gram_send.at[k], gram_recv.at[k, me], gram_ss.at[k, p], gram_rs.at[k, me], p)

        def into(i):
            p = (me + i) % n
            return remote(gram_send.at[k], gram_recv.at[k, p], gram_ss.at[k, p], gram_rs.at[k, p], p)

        each(1, n, lambda i: out(i).start())
        gram_recv[k, me] = packed
        each(1, n, lambda i: into(i).wait_recv())
        full = jnp.sum(gram_recv[k], axis=0)
        late.append(lambda: each(1, n, lambda i: out(i).wait_send()))
        parts = [full] + [pltpu.roll(full, LANES - g * vectors, 1) for g in range(1, vectors // SUB)]
        return jnp.where(lane32 < vectors, jnp.concatenate(parts, axis=0), 0.0)

    def gathered_dot(step, target):
        def along(i):
            return (far + i) % outer

        def across(k):
            return (near + k) % inner

        def ag_in(i):
            o = device(along(i), near, core)
            return remote(blk.at[step, o], blk.at[step, o], ag_ss.at[step, along(i)], ag_rs.at[step, along(i)], o)

        def row_out(i, k):
            o = device(along(i), near, core)
            return remote(blk.at[step, o], blk.at[step, o], row_ss.at[step, along(i), across(k)],
                          row_rs.at[step, along(i), near], device(far, across(k), core))

        def row_in(i, k):
            o = device(along(i), across(k), core)
            return remote(blk.at[step, o], blk.at[step, o], row_ss.at[step, along(i), across(k)],
                          row_rs.at[step, along(i), across(k)], device(far, across(k), core))

        def forward(i, k, side):
            a, b = along(i), across(k)
            o = device(a, b, side)
            return remote(blk.at[step, o], blk.at[step, o], fw_ss.at[step, a, b], fw_rs.at[step, a, b], partner)

        def add(acc, o):
            return acc + jnp.dot(blk[step, o], target[share_of(o), :], preferred_element_type=jnp.float32)

        def one(i, acc):
            @pl.when(i > 0)
            def _():
                ag_in(i).wait_recv()

            each(1, inner, lambda k: row_out(i, k).start())
            forward(i, 0, core).start()
            return add(acc, device(along(i), near, core))

        def two(i, acc):
            def inner_two(k, acc):
                row_in(i, k).wait_recv()
                forward(i, k, core).start()
                return add(acc, device(along(i), across(k), core))

            return lax.fori_loop(1, inner, inner_two, acc)

        def other(i, acc):
            def inner_other(k, acc):
                forward(i, k, 1 - core).wait_recv()
                return add(acc, device(along(i), across(k), 1 - core))

            return lax.fori_loop(0, inner, inner_other, acc)

        acc = lax.fori_loop(0, outer, one, jnp.zeros((vectors, steps), jnp.float32))
        acc = lax.fori_loop(0, outer, two, acc)
        acc = lax.fori_loop(0, outer, other, acc)

        def finish():
            @pl.loop(0, outer)
            def _(i):
                each(1, inner, lambda k: row_out(i, k).wait_send())
                each(0, inner, lambda k: forward(i, k, core).wait_send())

        late.append(finish)
        return acc

    for step in range(ITERS):
        if step == 0:
            def first_scores(p, acc):
                return acc + jnp.dot(
                    start_ref[:, share_of(p)], sparse[share_of(p), :], preferred_element_type=jnp.float32
                )

            scores = lax.fori_loop(0, n, first_scores, jnp.zeros((vectors, steps), jnp.float32))
        else:
            scores = gathered_dot(step - 1, sparse)
        scores = scores.astype(jnp.bfloat16)

        def image_of(p):
            return lax.dot_general(scores, sparse[share_of(p), :], NT, preferred_element_type=jnp.float32)

        def along(i):
            return (far + 1 + i) % outer

        def across(k):
            return (near + k) % inner

        def one_copy(i, k, step=step):
            a, b = along(i), across(k)
            return remote(one_send.at[a, b], one_recv.at[step, a, b], one_ss.at[step, a, b],
                          one_rs.at[step, a, b], partner)

        def near_copy(i, k, step=step):
            a, b = along(i), across(k)
            return remote(near_send.at[a, b], near_recv.at[step, a, near], near_ss.at[step, a, b],
                          near_rs.at[step, a, near], device(far, b, core))

        def near_from(i, k):
            a, b = along(i), across(k)
            return remote(near_send.at[a, b], near_recv.at[step, a, b], near_ss.at[step, a, b],
                          near_rs.at[step, a, b], device(far, b, core))

        def far_copy(i, step=step):
            a = along(i)
            return remote(far_send.at[a], far_recv.at[step, far], far_ss.at[step, a], far_rs.at[step, far],
                          device(a, near, core))

        def far_from(i):
            a = along(i)
            return remote(far_send.at[a], far_recv.at[step, a], far_ss.at[step, a], far_rs.at[step, a],
                          device(a, near, core))

        for done in sent:
            done()
        sent.clear()

        def give(i, k):
            one_send[along(i), across(k)] = image_of(device(along(i), across(k), 1 - core))
            one_copy(i, k).start()

        def keep(i, k):
            own = image_of(device(along(i), across(k), core))
            one_copy(i, k).wait_recv()
            return own + one_recv[step, along(i), across(k)]

        pl.loop(1, inner)(lambda k: give(0, k))

        @pl.loop(0, outer)
        def _(i):
            @pl.when(i < outer - 1)
            def _():
                pl.loop(1, inner)(lambda k: give(i + 1, k))

            @pl.loop(1, inner)
            def _(k):
                near_send[along(i), across(k)] = keep(i, k)
                near_copy(i, k).start()

        pl.loop(0, outer)(lambda i: give(i, 0))

        @pl.loop(0, outer)
        def _(i):
            far_send[along(i)] = keep(i, 0)

        def gather_near(i):
            def add(k, acc):
                near_from(i, k).wait_recv()
                return acc + near_recv[step, along(i), across(k)]

            return lax.fori_loop(1, inner, add, far_send[along(i)])

        @pl.loop(0, outer - 1)
        def _(i):
            far_send[along(i)] = gather_near(i)
            far_copy(i).start()

        def add(i, acc):
            far_from(i).wait_recv()
            return acc + far_recv[step, along(i)]

        image = lax.fori_loop(0, outer - 1, add, gather_near(outer - 1))

        def finish(one_copy=one_copy, near_copy=near_copy, far_copy=far_copy):
            @pl.loop(0, outer)
            def _(i):
                each(0, inner, lambda k: one_copy(i, k).wait_send())
                each(1, inner, lambda k: near_copy(i, k).wait_send())

            each(0, outer - 1, lambda i: far_copy(i).wait_send())

        sent.append(finish)

        inverse = inverse_factor(sum_gram(2 * step, image))
        first = jnp.dot(inverse, image, precision=HIGHEST, preferred_element_type=jnp.float32)
        inverse = inverse_factor(sum_gram(2 * step + 1, first))
        basis = jnp.dot(inverse, first, precision=HIGHEST, preferred_element_type=jnp.float32)
        blk[step, me] = basis.astype(jnp.bfloat16)

        def ag_copy(i, step=step):
            a = (far + i) % outer
            return remote(blk.at[step, me], blk.at[step, me], ag_ss.at[step, a], ag_rs.at[step, far],
                          device(a, near, core))

        each(1, outer, lambda i: ag_copy(i).start())
        late.append(lambda ag_copy=ag_copy: each(1, outer, lambda i: ag_copy(i).wait_send()))
        if step == ITERS - 1:
            basis_ref[...] = basis
            proj_ref[...] = gathered_dot(step, cusum)

    for done in sent + late:
        done()
    each(1, n, lambda i: tot_copy(i).wait_send())
    each(1, n, lambda i: bt_copy(i).wait_send())


def body(series, start_block):
    series_count, blocks = series.shape
    vectors = start_block.shape[0]
    n = lax.axis_size("tm")
    share = series_count // n
    tiles = share // LANES
    half = n // 2
    inner = 1
    while 4 * inner * inner <= half:
        inner *= 2
    outer = half // inner

    f32, bf16 = jnp.float32, jnp.bfloat16
    vmem = pl.BlockSpec(memory_space=pltpu.VMEM)
    dma = pltpu.SemaphoreType.DMA
    hbm = pl.BlockSpec(memory_space=pl.ANY)
    return pl.pallas_call(
        functools.partial(kernel, n, inner),
        out_shape=(
            jax.ShapeDtypeStruct((vectors, share), f32),
            jax.ShapeDtypeStruct((vectors, blocks), f32),
        ),
        in_specs=[hbm] * 2,
        out_specs=(vmem, vmem),
        scratch_shapes=[
            pltpu.VMEM((series_count, blocks), bf16),
            pltpu.VMEM((vectors, series_count), bf16),
            dma((n + 1,)),
            pltpu.VMEM((series_count, blocks), bf16),
            pltpu.VMEM((series_count, blocks), bf16),
            pltpu.VMEM((LANES, LANES), bf16),
            pltpu.VMEM((blocks, blocks), bf16),
            pltpu.VMEM((tiles, LANES, blocks), bf16),
            pltpu.VMEM((n, SUB, LANES), f32),
            pltpu.VMEM((n, SUB, LANES), f32),
            pltpu.VMEM((n, 2, SUB, LANES), f32),
            pltpu.VMEM((n, 2, SUB, LANES), f32),
            pltpu.VMEM((outer, inner, vectors, share), f32),
            pltpu.VMEM((ITERS, outer, inner, vectors, share), f32),
            pltpu.VMEM((outer, inner, vectors, share), f32),
            pltpu.VMEM((ITERS, outer, inner, vectors, share), f32),
            pltpu.VMEM((outer, vectors, share), f32),
            pltpu.VMEM((ITERS, outer, vectors, share), f32),
            pltpu.VMEM((2 * ITERS, SUB, LANES), f32),
            pltpu.VMEM((2 * ITERS, n, SUB, LANES), f32),
            pltpu.VMEM((ITERS, n, vectors, share), bf16),
            dma((n,)), dma((n,)), dma((n,)), dma((n,)),
            dma((ITERS, outer, inner)), dma((ITERS, outer, inner)),
            dma((ITERS, outer, inner)), dma((ITERS, outer, inner)),
            dma((ITERS, outer)), dma((ITERS, outer)),
            dma((2 * ITERS, n)), dma((2 * ITERS, n)),
            dma((ITERS, outer)), dma((ITERS, outer)),
            dma((ITERS, outer, inner)), dma((ITERS, outer, inner)),
            dma((ITERS, outer, inner)), dma((ITERS, outer, inner)),
        ],
        compiler_params=pltpu.CompilerParams(
            collective_id=0, has_side_effects=True, vmem_limit_bytes=56 * 1024 * 1024
        ),
        cost_estimate=pl.CostEstimate(
            flops=2 * series_count * blocks * (blocks + 6 * vectors), bytes_accessed=series_count * blocks * 2,
            transcendentals=0,
        ),
    )(series, start_block)


def solution(mesh):
    in_specs = (P("grp", "tm"), P())
    out_specs = (P(None, ("grp", "tm")), P(None, ("grp", "tm")))
    return jax.shard_map(body, mesh=mesh, in_specs=in_specs, out_specs=out_specs, check_vma=False)
```

```python
import functools

import jax
import jax.numpy as jnp
from jax import lax
from jax.experimental import pallas as pl
from jax.experimental.pallas import tpu as pltpu
from jax.sharding import PartitionSpec as P

ITERS = 2
THRESH = 1.0
LANES = 128
SUB = 8
MESH = pl.DeviceIdType.MESH
HIGHEST = lax.Precision.HIGHEST
NT = (((1,), (1,)), ((), ()))


def remote(src, dst, send_sem, recv_sem, peer):
    return pltpu.make_async_remote_copy(
        src_ref=src, dst_ref=dst, send_sem=send_sem, recv_sem=recv_sem,
        device_id={"tm": peer}, device_id_type=MESH,
    )


def each(low, high, run):
    if high - low <= 16:
        for i in range(low, high):
            run(i)
    else:
        pl.loop(low, high)(run)


def fold(low, high, run, state):
    if high - low <= 16:
        for i in range(low, high):
            state = run(i, state)
        return state
    return lax.fori_loop(low, high, run, state)


def inverse_factor(gram):
    width = gram.shape[0]
    rows = lax.broadcasted_iota(jnp.int32, (width, LANES), 0)
    cols = lax.broadcasted_iota(jnp.int32, (width, LANES), 1)
    eye = (rows == cols).astype(jnp.float32)
    trace = jnp.sum(jnp.sum(gram * eye, axis=1, keepdims=True), axis=0, keepdims=True)
    amount = 1e-05 * trace / width + 1e-06
    work = gram + amount * eye + (cols == rows + width).astype(jnp.float32)
    pivots = jnp.zeros((width, 1), jnp.float32)
    for j in range(width):
        top = work[j : j + 1, :]
        pivot = top[:, j : j + 1]
        column = work[:, j : j + 1]
        below = lax.broadcasted_iota(jnp.int32, (width, 1), 0)
        factor = jnp.where(below > j, column / pivot, 0.0)
        pivots = jnp.where(below == j, pivot, pivots)
        work = work - factor * top
    inverse = pltpu.roll(work, LANES - width, 1) * lax.rsqrt(pivots)
    return inverse[:, :width]


def kernel(n, inner, series_hbm, start_hbm, basis_ref, proj_ref,
           series_ref, start_ref, load_sem, sparse, cusum, lhs, tri_ref, corr_ref, tot_send, tot_recv, bt_send, bt_recv,
           one_send, one_recv, near_send, near_recv, far_send, far_recv, gram_send, gram_recv, blk,
           tot_ss, tot_rs, bt_ss, bt_rs, one_ss, one_rs, near_ss, near_rs,
           far_ss, far_rs, gram_ss, gram_rs, ag_ss, ag_rs, row_ss, row_rs, fw_ss, fw_rs):
    total_rows, steps = series_hbm.shape
    vectors = start_ref.shape[0]
    share = total_rows // n
    tiles = share // LANES
    half = n // 2
    me = lax.axis_index("tm")
    core = me % 2
    chip = me // 2
    partner = me + 1 - 2 * core
    outer = half // inner
    near = chip % inner
    far = chip // inner

    def device(a, b, side):
        return 2 * (a * inner + b) + side

    def load(p):
        rows = pl.ds(pl.multiple_of(p * share, share), share)
        return pltpu.make_async_copy(series_hbm.at[rows, :], series_ref.at[rows, :], load_sem.at[p])

    load_start = pltpu.make_async_copy(start_hbm, start_ref, load_sem.at[n])
    each(0, n, lambda p: load(p).start())
    load_start.start()

    barrier = pltpu.get_barrier_semaphore()

    @pl.loop(1, n)
    def _(i):
        pl.semaphore_signal(barrier, inc=1, device_id={"tm": (me + i) % n}, device_id_type=MESH)

    steps_f = jnp.float32(steps * n)
    tri_rows = lax.broadcasted_iota(jnp.int32, (steps, steps), 0)
    tri_cols = lax.broadcasted_iota(jnp.int32, (steps, steps), 1)
    tri_ref[...] = (tri_rows <= tri_cols).astype(jnp.float32).astype(jnp.bfloat16)
    step_id = lax.broadcasted_iota(jnp.int32, (1, steps), 1) + 1
    t_local = (me * steps + step_id).astype(jnp.float32)
    weight = jnp.where(
        t_local < steps_f, jnp.sqrt(steps_f / jnp.maximum(t_local * (steps_f - t_local), 1.0)), 0.0
    )
    coarse = -(jnp.zeros((1, steps), jnp.int32) + me * steps).astype(jnp.float32) / steps_f
    fine = -step_id.astype(jnp.float32) / steps_f
    kind = lax.broadcasted_iota(jnp.int32, (LANES, steps), 0)
    values = jnp.where(kind < 3 * SUB, 1.0, jnp.where(kind < 6 * SUB, coarse, fine))
    for q in range(tiles):
        used = (kind % SUB == q) & (kind < 9 * SUB)
        corr_ref[q] = jnp.where(used, values, 0.0).astype(jnp.bfloat16)

    ones = jnp.ones((SUB, steps), jnp.bfloat16)
    row8 = lax.broadcasted_iota(jnp.int32, (SUB, LANES), 0)

    @pl.loop(0, n)
    def _(p):
        load(p).wait()
        part = series_ref[pl.ds(pl.multiple_of(p * share, share), share), :]
        sums = lax.dot_general(ones, part, NT, preferred_element_type=jnp.float32)
        tile = jnp.zeros((SUB, LANES), jnp.float32)
        for q in range(tiles):
            tile = jnp.where(row8 == q, sums[:, q * LANES : (q + 1) * LANES], tile)
        tot_send[p] = tile

    pl.semaphore_wait(barrier, n - 1)

    def tot_copy(i):
        p = (me + i) % n
        return remote(tot_send.at[p], tot_recv.at[me], tot_ss.at[p], tot_rs.at[me], p)

    def tot_from(i):
        p = (me + i) % n
        return remote(tot_send.at[p], tot_recv.at[p], tot_ss.at[p], tot_rs.at[p], p)

    each(1, n, lambda i: tot_copy(i).start())
    tot_recv[me] = tot_send[me]
    each(1, n, lambda i: tot_from(i).wait_recv())

    def running(d, state):
        bt_send[d, 0] = state
        return state + tot_recv[d]

    total = fold(0, n, running, jnp.zeros((SUB, LANES), jnp.float32))

    def bt_copy(i):
        p = (me + i) % n
        return remote(bt_send.at[p], bt_recv.at[me], bt_ss.at[p], bt_rs.at[me], p)

    def bt_from(p):
        return remote(bt_send.at[p], bt_recv.at[p], bt_ss.at[p], bt_rs.at[p], p)

    def send_back(i):
        bt_send[(me + i) % n, 1] = total
        bt_copy(i).start()

    each(1, n, send_back)

    bt_send[me, 1] = total
    bt_recv[me] = bt_send[me]

    def pieces(value):
        high = value.astype(jnp.bfloat16).astype(jnp.float32)
        rest = value - high
        mid = rest.astype(jnp.bfloat16).astype(jnp.float32)
        return [high, mid, rest - mid]

    load_start.wait()

    def transform(i, acc):
        p = (me + i) % n

        @pl.when(i > 0)
        def _():
            bt_from(p).wait_recv()

        both = bt_recv[p]
        before, whole = pieces(both[0]), pieces(both[1])
        zero = jnp.zeros((SUB, LANES), jnp.float32)
        stack = jnp.concatenate(before + whole + whole + [zero] * 7, axis=0)
        lhs[...] = stack.T.astype(jnp.bfloat16)

        for q in range(tiles):
            rows = pl.ds(pl.multiple_of(p * share + q * LANES, LANES), LANES)
            prefix = jnp.dot(series_ref[rows, :], tri_ref[...], preferred_element_type=jnp.float32)
            prefix += jnp.dot(lhs[...], corr_ref[q], preferred_element_type=jnp.float32)
            raw = weight * prefix
            cusum[rows, :] = raw.astype(jnp.bfloat16)
            soft = raw - jnp.clip(raw, -THRESH, THRESH)
            soft = soft.astype(jnp.bfloat16)
            sparse[rows, :] = soft
        return acc

    lax.fori_loop(0, n, transform, 0)

    def share_of(p):
        return pl.ds(pl.multiple_of(p * share, share), share)

    late = []
    sent = []
    lane32 = lax.broadcasted_iota(jnp.int32, (vectors, LANES), 1)

    def sum_gram(k, value):
        part = lax.dot_general(value, value, NT, precision=HIGHEST, preferred_element_type=jnp.float32)
        wide = jnp.concatenate([part] * (LANES // vectors), axis=1)
        packed = jnp.zeros((SUB, LANES), jnp.float32)
        lane8 = lax.broadcasted_iota(jnp.int32, (SUB, LANES), 1) // vectors
        for g in range(vectors // SUB):
            packed = jnp.where(lane8 == g, wide[g * SUB : (g + 1) * SUB, :], packed)
        gram_send[k] = packed

        def out(i):
            p = (me + i) % n
            return remote(gram_send.at[k], gram_recv.at[k, me], gram_ss.at[k, p], gram_rs.at[k, me], p)

        def into(i):
            p = (me + i) % n
            return remote(gram_send.at[k], gram_recv.at[k, p], gram_ss.at[k, p], gram_rs.at[k, p], p)

        each(1, n, lambda i: out(i).start())
        gram_recv[k, me] = packed
        each(1, n, lambda i: into(i).wait_recv())
        full = jnp.sum(gram_recv[k], axis=0)
        late.append(lambda: each(1, n, lambda i: out(i).wait_send()))
        parts = [full] + [pltpu.roll(full, LANES - g * vectors, 1) for g in range(1, vectors // SUB)]
        return jnp.where(lane32 < vectors, jnp.concatenate(parts, axis=0), 0.0)

    def gathered_dot(step, target):
        def along(i):
            return (far + i) % outer

        def across(k):
            return (near + k) % inner

        def ag_in(i):
            o = device(along(i), near, core)
            return remote(blk.at[step, o], blk.at[step, o], ag_ss.at[step, along(i)], ag_rs.at[step, along(i)], o)

        def row_out(i, k):
            o = device(along(i), near, core)
            return remote(blk.at[step, o], blk.at[step, o], row_ss.at[step, along(i), across(k)],
                          row_rs.at[step, along(i), near], device(far, across(k), core))

        def row_in(i, k):
            o = device(along(i), across(k), core)
            return remote(blk.at[step, o], blk.at[step, o], row_ss.at[step, along(i), across(k)],
                          row_rs.at[step, along(i), across(k)], device(far, across(k), core))

        def forward(i, k, side):
            a, b = along(i), across(k)
            o = device(a, b, side)
            return remote(blk.at[step, o], blk.at[step, o], fw_ss.at[step, a, b], fw_rs.at[step, a, b], partner)

        def add(acc, o):
            return acc + jnp.dot(blk[step, o], target[share_of(o), :], preferred_element_type=jnp.float32)

        def one(i, acc):
            @pl.when(i > 0)
            def _():
                ag_in(i).wait_recv()

            each(1, inner, lambda k: row_out(i, k).start())
            forward(i, 0, core).start()
            return add(acc, device(along(i), near, core))

        def two(i, acc):
            def inner_two(k, acc):
                row_in(i, k).wait_recv()
                forward(i, k, core).start()
                return add(acc, device(along(i), across(k), core))

            return lax.fori_loop(1, inner, inner_two, acc)

        def other(i, acc):
            def inner_other(k, acc):
                forward(i, k, 1 - core).wait_recv()
                return add(acc, device(along(i), across(k), 1 - core))

            return lax.fori_loop(0, inner, inner_other, acc)

        acc = lax.fori_loop(0, outer, one, jnp.zeros((vectors, steps), jnp.float32))
        acc = lax.fori_loop(0, outer, two, acc)
        acc = lax.fori_loop(0, outer, other, acc)

        def finish():
            @pl.loop(0, outer)
            def _(i):
                each(1, inner, lambda k: row_out(i, k).wait_send())
                each(0, inner, lambda k: forward(i, k, core).wait_send())

        late.append(finish)
        return acc

    for step in range(ITERS):
        if step == 0:
            def first_scores(p, acc):
                return acc + jnp.dot(
                    start_ref[:, share_of(p)], sparse[share_of(p), :], preferred_element_type=jnp.float32
                )

            scores = fold(0, n, first_scores, jnp.zeros((vectors, steps), jnp.float32))
        else:
            scores = gathered_dot(step - 1, sparse)
        scores = scores.astype(jnp.bfloat16)

        def image_of(p):
            return lax.dot_general(scores, sparse[share_of(p), :], NT, preferred_element_type=jnp.float32)

        def along(i):
            return (far + 1 + i) % outer

        def across(k):
            return (near + k) % inner

        def one_copy(i, k, step=step):
            a, b = along(i), across(k)
            return remote(one_send.at[a, b], one_recv.at[step, a, b], one_ss.at[step, a, b],
                          one_rs.at[step, a, b], partner)

        def near_copy(i, k, step=step):
            a, b = along(i), across(k)
            return remote(near_send.at[a, b], near_recv.at[step, a, near], near_ss.at[step, a, b],
                          near_rs.at[step, a, near], device(far, b, core))

        def near_from(i, k):
            a, b = along(i), across(k)
            return remote(near_send.at[a, b], near_recv.at[step, a, b], near_ss.at[step, a, b],
                          near_rs.at[step, a, b], device(far, b, core))

        def far_copy(i, step=step):
            a = along(i)
            return remote(far_send.at[a], far_recv.at[step, far], far_ss.at[step, a], far_rs.at[step, far],
                          device(a, near, core))

        def far_from(i):
            a = along(i)
            return remote(far_send.at[a], far_recv.at[step, a], far_ss.at[step, a], far_rs.at[step, a],
                          device(a, near, core))

        for done in sent:
            done()
        sent.clear()

        def give(i, k):
            one_send[along(i), across(k)] = image_of(device(along(i), across(k), 1 - core))
            one_copy(i, k).start()

        def keep(i, k):
            own = image_of(device(along(i), across(k), core))
            one_copy(i, k).wait_recv()
            return own + one_recv[step, along(i), across(k)]

        pl.loop(1, inner)(lambda k: give(0, k))

        @pl.loop(0, outer)
        def _(i):
            @pl.when(i < outer - 1)
            def _():
                pl.loop(1, inner)(lambda k: give(i + 1, k))

            @pl.loop(1, inner)
            def _(k):
                near_send[along(i), across(k)] = keep(i, k)
                near_copy(i, k).start()

        each(0, outer, lambda i: give(i, 0))

        @pl.loop(0, outer)
        def _(i):
            far_send[along(i)] = keep(i, 0)

        def gather_near(i):
            def add(k, acc):
                near_from(i, k).wait_recv()
                return acc + near_recv[step, along(i), across(k)]

            return lax.fori_loop(1, inner, add, far_send[along(i)])

        @pl.loop(0, outer - 1)
        def _(i):
            far_send[along(i)] = gather_near(i)
            far_copy(i).start()

        def add(i, acc):
            far_from(i).wait_recv()
            return acc + far_recv[step, along(i)]

        image = lax.fori_loop(0, outer - 1, add, gather_near(outer - 1))

        def finish(one_copy=one_copy, near_copy=near_copy, far_copy=far_copy):
            @pl.loop(0, outer)
            def _(i):
                each(0, inner, lambda k: one_copy(i, k).wait_send())
                each(1, inner, lambda k: near_copy(i, k).wait_send())

            each(0, outer - 1, lambda i: far_copy(i).wait_send())

        sent.append(finish)

        inverse = inverse_factor(sum_gram(2 * step, image))
        first = jnp.dot(inverse, image, precision=HIGHEST, preferred_element_type=jnp.float32)
        inverse = inverse_factor(sum_gram(2 * step + 1, first))
        basis = jnp.dot(inverse, first, precision=HIGHEST, preferred_element_type=jnp.float32)
        blk[step, me] = basis.astype(jnp.bfloat16)

        def ag_copy(i, step=step):
            a = (far + i) % outer
            return remote(blk.at[step, me], blk.at[step, me], ag_ss.at[step, a], ag_rs.at[step, far],
                          device(a, near, core))

        each(1, outer, lambda i: ag_copy(i).start())
        late.append(lambda ag_copy=ag_copy: each(1, outer, lambda i: ag_copy(i).wait_send()))
        if step == ITERS - 1:
            basis_ref[...] = basis
            proj_ref[...] = gathered_dot(step, cusum)

    for done in sent + late:
        done()
    each(1, n, lambda i: tot_copy(i).wait_send())
    each(1, n, lambda i: bt_copy(i).wait_send())


def body(series, start_block):
    series_count, blocks = series.shape
    vectors = start_block.shape[0]
    n = lax.axis_size("tm")
    share = series_count // n
    tiles = share // LANES
    half = n // 2
    inner = 1
    while 4 * inner * inner <= half:
        inner *= 2
    outer = half // inner

    f32, bf16 = jnp.float32, jnp.bfloat16
    vmem = pl.BlockSpec(memory_space=pltpu.VMEM)
    dma = pltpu.SemaphoreType.DMA
    hbm = pl.BlockSpec(memory_space=pl.ANY)
    return pl.pallas_call(
        functools.partial(kernel, n, inner),
        out_shape=(
            jax.ShapeDtypeStruct((vectors, share), f32),
            jax.ShapeDtypeStruct((vectors, blocks), f32),
        ),
        in_specs=[hbm] * 2,
        out_specs=(vmem, vmem),
        scratch_shapes=[
            pltpu.VMEM((series_count, blocks), bf16),
            pltpu.VMEM((vectors, series_count), bf16),
            dma((n + 1,)),
            pltpu.VMEM((series_count, blocks), bf16),
            pltpu.VMEM((series_count, blocks), bf16),
            pltpu.VMEM((LANES, LANES), bf16),
            pltpu.VMEM((blocks, blocks), bf16),
            pltpu.VMEM((tiles, LANES, blocks), bf16),
            pltpu.VMEM((n, SUB, LANES), f32),
            pltpu.VMEM((n, SUB, LANES), f32),
            pltpu.VMEM((n, 2, SUB, LANES), f32),
            pltpu.VMEM((n, 2, SUB, LANES), f32),
            pltpu.VMEM((outer, inner, vectors, share), f32),
            pltpu.VMEM((ITERS, outer, inner, vectors, share), f32),
            pltpu.VMEM((outer, inner, vectors, share), f32),
            pltpu.VMEM((ITERS, outer, inner, vectors, share), f32),
            pltpu.VMEM((outer, vectors, share), f32),
            pltpu.VMEM((ITERS, outer, vectors, share), f32),
            pltpu.VMEM((2 * ITERS, SUB, LANES), f32),
            pltpu.VMEM((2 * ITERS, n, SUB, LANES), f32),
            pltpu.VMEM((ITERS, n, vectors, share), bf16),
            dma((n,)), dma((n,)), dma((n,)), dma((n,)),
            dma((ITERS, outer, inner)), dma((ITERS, outer, inner)),
            dma((ITERS, outer, inner)), dma((ITERS, outer, inner)),
            dma((ITERS, outer)), dma((ITERS, outer)),
            dma((2 * ITERS, n)), dma((2 * ITERS, n)),
            dma((ITERS, outer)), dma((ITERS, outer)),
            dma((ITERS, outer, inner)), dma((ITERS, outer, inner)),
            dma((ITERS, outer, inner)), dma((ITERS, outer, inner)),
        ],
        compiler_params=pltpu.CompilerParams(
            collective_id=0, has_side_effects=True, vmem_limit_bytes=56 * 1024 * 1024
        ),
        cost_estimate=pl.CostEstimate(
            flops=2 * series_count * blocks * (blocks + 6 * vectors), bytes_accessed=series_count * blocks * 2,
            transcendentals=0,
        ),
    )(series, start_block)


def solution(mesh):
    in_specs = (P("grp", "tm"), P())
    out_specs = (P(None, ("grp", "tm")), P(None, ("grp", "tm")))
    return jax.shard_map(body, mesh=mesh, in_specs=in_specs, out_specs=out_specs, check_vma=False)
```
